256 devices in a mesh: op: 32 (over y, x, core), grp: 8 (over z).
Axes of the slice: x: 4, y: 4, z: 8, core: 2. Of those that a mesh axis runs over, the one named last changes fastest.
Arguments:
- wavefunction: bfloat16 [8, 256, 256], P('grp'), may hold values from -6 to 6
- block_rows: int32 [8], P('grp'), may hold values from 128 to 256
- left_terms: bfloat16 [12288, 256, 256], P(('op', 'grp')), may hold values from -0.375 to 0.375
- right_terms: bfloat16 [12288, 256, 256], P(('op', 'grp')), may hold values from -0.013671875 to 0.013671875
- block_pairs: int32 [12288, 2], P(('op', 'grp')), may hold values from 0 to 7
- live_counts: int32 [256], P(('op', 'grp')), may hold values from 1 to 48, 6144 in all
Outputs:
- sigma: float32 [8, 256, 256], P('grp', 'op')
The draws below stay inside these ranges and needn't reach their ends.
Inputs may be any that keep to these rules, and one draw needn't show every extreme that they name: `live_counts`: some device uses all 48 of its slots.
All inputs are finite; a program needn't handle non-finite values.
Results may differ from the reference program's by a relative error of at most 0.0029.
Values may be sent and summed in bfloat16 or wider, within the bound.
No kernel may reach another device: no remote copies, remote signals or barrier semaphores. Data moves between devices by JAX's collectives and lax.ppermute only.
A program may use at most 128 MiB of HBM per device.

```python
import math
import jax
import jax.numpy as jnp
import numpy as np
from jax import lax

BL = 256
BR = 256
BLK_DEV = 1
ENT_DEV = 48
NB = 8
ENT = 12288
N_OP = 32
N_GRP = 8


def place_ends(drawn, rng, least, top_value):
    longest = drawn.shape.index(max(drawn.shape))
    spots = []
    for shift in (0, 1):
        where = [jax.random.randint(jax.random.fold_in(rng, axis), (), 0, length) for axis, length in enumerate(drawn.shape)]
        where[longest] = (where[longest] + shift) % drawn.shape[longest]
        spots.append(tuple(where))
    return drawn.at[spots[0]].set(least).at[spots[1]].set(top_value)


def block_scale(key, shape, split, smallest, high):
    factor_of, own = 1.0, jax.random.fold_in(key, 6)
    for axis_at, parts in split:
        steps = jnp.exp(jax.random.uniform(jax.random.fold_in(own, axis_at), (parts,), jnp.float32, smallest / len(split), high / len(split)))
        factor_of = factor_of * jnp.repeat(steps, shape[axis_at] // parts).reshape([-1 if axis == axis_at else 1 for axis in range(len(shape))])
    return factor_of


def length_profile(number_of, total, bound, skew):
    weights = [(1 << 20) // math.isqrt(rank ** skew) + 1 for rank in range(2, number_of + 1)]
    rest, counts = total - bound - (number_of - 1), [1] * (number_of - 1)
    while rest > 0:
        movable = [i for i in range(number_of - 1) if counts[i] < bound]
        mass, left = sum([weights[i] for i in movable]), rest
        for i in movable:
            addition = min(bound - counts[i], max(1, left * weights[i] // mass), rest)
            counts[i] = counts[i] + addition
            rest = rest - addition
    return np.array([bound] + counts)


def ragged(stream_key, count, total, most, slope):
    if count == 2:
        one = jax.random.randint(stream_key, (), max(1, total - most), min(most, total - 1) + 1)
        return jnp.stack([one, total - one])
    sizes = jnp.asarray(length_profile(count, total, most, slope), jnp.int32)
    pairs = (count - 1) // 2
    donor, taker = sizes[1:1 + 2 * pairs:2], sizes[2:2 + 2 * pairs:2]
    room = jnp.minimum(donor - 1, most - taker)
    moved = jax.random.randint(jax.random.fold_in(stream_key, 1), (pairs,), 0, 1 << 20) % (room + 1)
    sizes = sizes.at[1:1 + 2 * pairs:2].set(donor - moved).at[2:2 + 2 * pairs:2].set(taker + moved)
    return sizes[jax.random.permutation(jax.random.fold_in(stream_key, 2), count)]


def normal_values(own_key, dims, width, reach, split=(), held_as=jnp.bfloat16):
    result = jax.random.normal(own_key, dims, jnp.float32) * width
    if len(split) > 0:
        result = block_scale(own_key, dims, split, -0.22, 0.18) * result
    return jnp.clip(result, min=-reach, max=reach).astype(held_as)


def setup_inputs(seed: int = 0) -> dict:
    arg_keys = jax.random.split(jax.random.key(seed), 7)
    wavefunction = normal_values(arg_keys[0], (NB, BL, BR), 1.0, 6.0, ((0, 8),))
    block_rows = place_ends(jax.random.randint(arg_keys[1], (NB,), BL // 2, BL + 1), jax.random.fold_in(arg_keys[1], 1), BL // 2, BL).astype(jnp.int32)
    left_terms = normal_values(arg_keys[2], (ENT, BL, BL), BL ** -0.5, 0.375, ((0, 256),))
    right_terms = normal_values(arg_keys[3], (ENT, BR, BR), (BR * ENT_DEV * N_OP // (2 * BLK_DEV)) ** -0.5, 0.013671875, ((0, 256),))
    block_pairs = place_ends(jax.random.randint(arg_keys[4], (ENT, 2), 0, NB), jax.random.fold_in(arg_keys[4], 1), 0, NB - 1).astype(jnp.int32)
    live_counts = ragged(arg_keys[5], N_OP * N_GRP, N_OP * N_GRP * ENT_DEV // 2, ENT_DEV, 2).astype(jnp.int32)
    return dict(wavefunction=wavefunction, block_rows=block_rows, left_terms=left_terms, right_terms=right_terms, block_pairs=block_pairs, live_counts=live_counts)


def reference(wavefunction, block_rows, left_terms, right_terms, block_pairs, live_counts):
    row_index = lax.broadcasted_iota(jnp.int32, wavefunction.shape, 1)
    keep_rows = row_index < block_rows.astype(jnp.int32)[:, None, None]
    masked = jnp.where(keep_rows, wavefunction, jnp.zeros_like(wavefunction))
    total_entries = left_terms.shape[0]
    per_device = total_entries // live_counts.shape[0]

    def add_entry(position, totals):
        owner = position // per_device
        live_now = (position % per_device) < live_counts[owner]

        def contribute(sums):
            source = block_pairs[position, 0].astype(jnp.int32)
            target = block_pairs[position, 1].astype(jnp.int32)
            source_block = lax.dynamic_index_in_dim(masked, source, 0, keepdims=False)
            left_product = jnp.dot(left_terms[position], source_block, preferred_element_type=jnp.float32).astype(jnp.bfloat16)
            contribution = jnp.dot(left_product, right_terms[position], preferred_element_type=jnp.float32)
            previous = lax.dynamic_index_in_dim(sums, target, 0, keepdims=False)
            return lax.dynamic_update_index_in_dim(sums, previous + contribution, target, 0)

        return lax.cond(live_now, contribute, lambda sums: sums, totals)

    zeros_block = jnp.zeros(wavefunction.shape, jnp.float32)
    summed = lax.fori_loop(0, total_entries, add_entry, zeros_block)
    return jnp.where(keep_rows, summed, jnp.zeros_like(summed))
```

```python
import jax
import jax.numpy as jnp
from jax import lax
from jax.experimental import pallas as pl
from jax.experimental.pallas import tpu as pltpu
from jax.sharding import Mesh, PartitionSpec as P

GROUP = 8
LAYER = ("y", "x")
SWAP = [(0, 1), (1, 0)]


def term_kernel(
    core_ref, live_ref, pairs_ref, mine_ref, other_ref, left, right, keep_ref, send_ref,
    psi, acc, psi_sem, out_sem,
):
    core, live = core_ref[0], live_ref[0]
    blocks, half, width = mine_ref.shape
    tiles, share, _ = send_ref.shape
    mine_rows = pl.ds(pl.multiple_of(core * half, half), half)
    other_rows = pl.ds(pl.multiple_of((1 - core) * half, half), half)
    loads = [
        pltpu.make_async_copy(mine_ref, psi.at[:, mine_rows], psi_sem.at[0]),
        pltpu.make_async_copy(other_ref, psi.at[:, other_rows], psi_sem.at[1]),
    ]
    for load in loads:
        load.start()
    acc[...] = jnp.zeros_like(acc)
    for load in loads:
        load.wait()

    def step(j, carry):
        products = []
        for i in range(GROUP):
            k = j * GROUP + i
            product = jnp.dot(left[k], psi[pairs_ref[k, 0]], preferred_element_type=jnp.float32)
            products.append(product.astype(jnp.bfloat16))
        for i in range(GROUP):
            k = j * GROUP + i
            target = jnp.where(k < live, pairs_ref[k, 1], blocks)
            term = jnp.dot(products[i], right[k], preferred_element_type=jnp.float32)
            term = term.reshape(tiles, 2, 8, width)
            for c in range(2):
                acc[c, :, target] += term[:, c]
        return carry

    lax.fori_loop(0, (live + GROUP - 1) // GROUP, step, 0)
    for tile in range(tiles):
        sums = acc[1 - core, tile, :blocks].reshape(share, width)
        send_ref[tile] = sums.astype(send_ref.dtype)
    keep = pltpu.make_async_copy(acc.at[core, :, :blocks], keep_ref, out_sem)
    keep.start()
    keep.wait()


def term_sums(core, live, pairs, mine, other, left, right):
    slots, rows, width = left.shape
    blocks = mine.shape[0]
    tiles = rows // 16
    smem = pl.BlockSpec(memory_space=pltpu.SMEM)
    vmem = pl.BlockSpec(memory_space=pltpu.VMEM)
    anywhere = pl.BlockSpec(memory_space=pl.ANY)
    return pl.pallas_call(
        term_kernel,
        out_shape=(
            jax.ShapeDtypeStruct((tiles, blocks, 8, width), jnp.float32),
            jax.ShapeDtypeStruct((tiles, blocks * 8, width), jnp.bfloat16),
        ),
        in_specs=[smem, smem, smem, anywhere, anywhere, vmem, vmem],
        out_specs=(anywhere, vmem),
        scratch_shapes=[
            pltpu.VMEM((blocks, rows, width), jnp.bfloat16),
            pltpu.VMEM((2, tiles, blocks + 1, 8, width), jnp.float32),
            pltpu.SemaphoreType.DMA((2,)),
            pltpu.SemaphoreType.DMA,
        ],
        compiler_params=pltpu.CompilerParams(vmem_limit_bytes=24 * 1024 * 1024),
        cost_estimate=pl.CostEstimate(
            flops=4 * rows * rows * width * slots,
            bytes_accessed=4 * rows * width * slots,
            transcendentals=0,
        ),
    )(core, live, pairs, mine, other, left, right)


def body(wavefunction, block_rows, left_terms, right_terms, block_pairs, live_counts):
    _, rows, width = wavefunction.shape
    core = lax.axis_index("c").astype(jnp.int32)
    blocks = lax.axis_size("z")
    half = rows // 2
    own_half = lax.dynamic_slice_in_dim(wavefunction[0], core * half, half, 0)
    row_index = core * half + lax.broadcasted_iota(jnp.int32, (half, 1), 0)
    masked = jnp.where(row_index < block_rows[0], own_half, jnp.zeros_like(own_half))
    mine = lax.all_to_all(jnp.broadcast_to(masked, (blocks, half, width)), "z", 0, 0)
    other = lax.ppermute(mine, "c", SWAP)
    keep, send = term_sums(
        core[None], live_counts, block_pairs, mine, other, left_terms, right_terms
    )
    received = lax.ppermute(send, "c", SWAP)
    tiles = keep.shape[0]
    pair_sum = keep.reshape(tiles, blocks * 8, width) + received.astype(jnp.float32)
    pieces = lax.all_to_all(pair_sum.astype(jnp.bfloat16), LAYER, 0, 0)
    layer_sum = pieces.astype(jnp.float32).sum(0).reshape(blocks, 8, width)
    sigma = lax.all_to_all(layer_sum, "z", 0, 0).sum(0)
    own_tile = lax.axis_index(("y", "x", "c"))
    own_rows = own_tile * 8 + lax.broadcasted_iota(jnp.int32, (8, 1), 0)
    return jnp.where(own_rows < block_rows[0], sigma, jnp.zeros_like(sigma))[None]


def solution(mesh):
    devices = mesh.devices.reshape(4, 4, 2, mesh.shape["grp"])
    grid = Mesh(devices, ("y", "x", "c", "z"))
    everywhere = ("y", "x", "c", "z")
    placed = (
        P("z", None, None),
        P("z"),
        P(everywhere, None, None),
        P(everywhere, None, None),
        P(everywhere, None),
        P(everywhere),
    )
    return jax.shard_map(
        body, mesh=grid, in_specs=placed, out_specs=P("z", ("y", "x", "c"), None), check_vma=False
    )
```

```python
import jax
import jax.numpy as jnp
from jax import lax
from jax.experimental import pallas as pl
from jax.experimental.pallas import tpu as pltpu
from jax.sharding import Mesh, PartitionSpec as P

GROUP = 8
PARTS = 4
LAYER = ("y", "x")
SWAP = [(0, 1), (1, 0)]
SMEM = pl.BlockSpec(memory_space=pltpu.SMEM)
VMEM = pl.BlockSpec(memory_space=pltpu.VMEM)


def prepare_kernel(
    place_ref, live_ref, pairs_ref, left_ref, right_ref,
    lists_ref, counts_ref, left_here, right_here, left_sem, right_sem,
):
    part = left_ref.shape[0] // PARTS
    loads = []
    for i in range(PARTS):
        slots = pl.ds(i * part, part)
        loads.append(
            pltpu.make_async_copy(left_ref.at[slots], left_here.at[slots], left_sem.at[i])
        )
        loads.append(
            pltpu.make_async_copy(right_ref.at[slots], right_here.at[slots], right_sem.at[i])
        )
    for load in loads:
        load.start()
    core, layer = place_ref[0], place_ref[1]

    def clear(i, carry):
        for which in range(2):
            lists_ref[which, 0, i] = 0
            lists_ref[which, 1, i] = 0
            lists_ref[which, 2, i] = 8
        return carry

    lax.fori_loop(0, lists_ref.shape[2], clear, 0)

    def place(k, counts):
        ahead = (pairs_ref[0, k] - layer) & 7
        hops = jnp.minimum(ahead, 8 - ahead)
        behind = (ahead > 4).astype(jnp.int32)
        theirs = jnp.where(hops == 0, 0, jnp.where(hops == 4, 1, 1 - (behind ^ core)))
        at = jnp.where(theirs == 0, counts[0], counts[1])
        lists_ref[theirs, 0, at] = k
        lists_ref[theirs, 1, at] = jnp.where(hops == 0, 0, 4 - hops)
        lists_ref[theirs, 2, at] = pairs_ref[1, k]
        return counts[0] + 1 - theirs, counts[1] + theirs

    first, second = lax.fori_loop(0, live_ref[0], place, (jnp.int32(0), jnp.int32(0)))
    counts_ref[0] = first
    counts_ref[1] = second
    for load in loads:
        load.wait()


def prepare(place, live, pairs, left, right):
    slots = pairs.shape[1]
    return pl.pallas_call(
        prepare_kernel,
        out_shape=(
            jax.ShapeDtypeStruct((2, 3, slots + GROUP), jnp.int32),
            jax.ShapeDtypeStruct((2,), jnp.int32),
            jax.ShapeDtypeStruct(left.shape, left.dtype),
            jax.ShapeDtypeStruct(right.shape, right.dtype),
        ),
        in_specs=[SMEM] * 3 + [pl.BlockSpec(memory_space=pl.ANY)] * 2,
        out_specs=(SMEM, SMEM, VMEM, VMEM),
        scratch_shapes=[pltpu.SemaphoreType.DMA((PARTS,)), pltpu.SemaphoreType.DMA((PARTS,))],
        compiler_params=pltpu.CompilerParams(vmem_limit_bytes=40 * 1024 * 1024),
        cost_estimate=pl.CostEstimate(
            flops=0, bytes_accessed=4 * (left.size + right.size), transcendentals=0
        ),
    )(place, live, pairs, left, right)


def add_terms(which, lists_ref, counts_ref, psi, left, right, acc):
    tiles, width = acc.shape[1], acc.shape[-1]

    def step(j, carry):
        products = []
        for i in range(GROUP):
            slot, source = lists_ref[which, 0, j * GROUP + i], lists_ref[which, 1, j * GROUP + i]
            block = psi[pl.ds(pl.multiple_of(source * width, width), width)]
            product = jnp.dot(left[slot], block, preferred_element_type=jnp.float32)
            products.append(product.astype(jnp.bfloat16))
        for i in range(GROUP):
            slot, target = lists_ref[which, 0, j * GROUP + i], lists_ref[which, 2, j * GROUP + i]
            term = jnp.dot(products[i], right[slot], preferred_element_type=jnp.float32)
            term = term.reshape(tiles, 2, 8, width)
            for c in range(2):
                acc[c, :, target] += term[:, c]
        return carry

    lax.fori_loop(0, (counts_ref[which] + GROUP - 1) // GROUP, step, 0)


def first_kernel(lists_ref, counts_ref, mine, left, right, acc):
    acc[...] = jnp.zeros_like(acc)
    add_terms(0, lists_ref, counts_ref, mine, left, right, acc)


def second_kernel(
    place_ref, lists_ref, counts_ref, mine, other, left, right, before, keep_ref, send_ref, psi, acc
):
    core = place_ref[0]
    tiles, share, width = send_ref.shape
    fetched, half = 4 * width, width // 2
    psi[width:fetched] = other[width:fetched]
    own_rows = pl.ds(pl.multiple_of(core * half, half), half)
    their_rows = pl.ds(pl.multiple_of((1 - core) * half, half), half)
    psi[own_rows] = mine[fetched : fetched + half]
    psi[their_rows] = other[fetched : fetched + half]
    acc[...] = before[...]
    add_terms(1, lists_ref, counts_ref, psi, left, right, acc)
    for tile in range(tiles):
        keep_ref[tile] = acc[core, tile, :8].reshape(share, width)
        send_ref[tile] = acc[1 - core, tile, :8].reshape(share, width).astype(send_ref.dtype)


def term_cost(left):
    slots, rows, width = left.shape
    return pl.CostEstimate(
        flops=2 * rows * rows * width * slots,
        bytes_accessed=2 * rows * width * slots,
        transcendentals=0,
    )


def first_terms(lists, counts, mine, left, right):
    _, rows, width = left.shape
    return pl.pallas_call(
        first_kernel,
        out_shape=jax.ShapeDtypeStruct((2, rows // 16, 9, 8, width), jnp.float32),
        in_specs=[SMEM] * 2 + [VMEM] * 3,
        out_specs=VMEM,
        compiler_params=pltpu.CompilerParams(vmem_limit_bytes=24 * 1024 * 1024),
        cost_estimate=term_cost(left),
    )(lists, counts, mine, left, right)


def second_terms(place, lists, counts, mine, other, left, right, before):
    _, rows, width = left.shape
    tiles = rows // 16
    return pl.pallas_call(
        second_kernel,
        out_shape=(
            jax.ShapeDtypeStruct((tiles, 64, width), jnp.float32),
            jax.ShapeDtypeStruct((tiles, 64, width), jnp.bfloat16),
        ),
        in_specs=[SMEM] * 3 + [VMEM] * 5,
        out_specs=(VMEM, VMEM),
        scratch_shapes=[
            pltpu.VMEM((4 * rows, width), jnp.bfloat16),
            pltpu.VMEM((2, tiles, 9, 8, width), jnp.float32),
        ],
        compiler_params=pltpu.CompilerParams(vmem_limit_bytes=24 * 1024 * 1024),
        cost_estimate=term_cost(left),
    )(place, lists, counts, mine, other, left, right, before)


def fetch(value, shifts):
    moves = [
        (core * 8 + layer, core * 8 + (layer + shift) % 8)
        for core, shift in enumerate(shifts)
        for layer in range(8)
    ]
    return lax.ppermute(value, ("c", "z"), moves)


def body(wavefunction, block_rows, left_terms, right_terms, block_pairs, live_counts):
    _, rows, width = wavefunction.shape
    core = lax.axis_index("c").astype(jnp.int32)
    layer = lax.axis_index("z").astype(jnp.int32)
    place = jnp.stack([core, layer])
    half = rows // 2
    row_index = lax.broadcasted_iota(jnp.int32, (rows, 1), 0)
    own = jnp.where(row_index < block_rows[0], wavefunction[0], jnp.zeros_like(wavefunction[0]))
    own_half = jnp.where(core == 0, own[:half], own[half:])
    fetched = [fetch(own, (shift, -shift)) for shift in (3, 2, 1)]
    far = fetch(own_half, (4, 4))
    lists, counts, left_terms, right_terms = prepare(
        place, live_counts, block_pairs.T, left_terms, right_terms
    )
    fetched, far, lists, counts, left_terms, right_terms = lax.optimization_barrier(
        (fetched, far, lists, counts, left_terms, right_terms)
    )
    mine = jnp.concatenate([own, *fetched, far], 0)
    other = lax.ppermute(mine, "c", SWAP)
    before = first_terms(lists, counts, mine, left_terms, right_terms)
    keep, send = second_terms(
        place, lists, counts, mine, other, left_terms, right_terms, before
    )
    received = lax.ppermute(send, "c", SWAP)
    pair_sum = keep + received.astype(jnp.float32)
    pieces = lax.all_to_all(pair_sum.astype(jnp.bfloat16), LAYER, 0, 0)
    layer_sum = pieces.astype(jnp.float32).sum(0).reshape(8, 8, width)
    sigma = lax.all_to_all(layer_sum, "z", 0, 0).sum(0)
    own_tile = lax.axis_index(("y", "x", "c"))
    own_rows = own_tile * 8 + lax.broadcasted_iota(jnp.int32, (8, 1), 0)
    return jnp.where(own_rows < block_rows[0], sigma, jnp.zeros_like(sigma))[None]


def solution(mesh):
    devices = mesh.devices.reshape(4, 4, 2, mesh.shape["grp"])
    grid = Mesh(devices, ("y", "x", "c", "z"))
    everywhere = ("y", "x", "c", "z")
    placed = (
        P("z", None, None),
        P("z"),
        P(everywhere, None, None),
        P(everywhere, None, None),
        P(everywhere, None),
        P(everywhere),
    )
    return jax.shard_map(
        body, mesh=grid, in_specs=placed, out_specs=P("z", ("y", "x", "c"), None), check_vma=False
    )
```

```python
import jax
import jax.numpy as jnp
from jax import lax
from jax.experimental import pallas as pl
from jax.experimental.pallas import tpu as pltpu
from jax.sharding import Mesh, PartitionSpec as P

GROUP = 8
PARTS = 6
LAYER = ("y", "x")
SWAP = [(0, 1), (1, 0)]
SMEM = pl.BlockSpec(memory_space=pltpu.SMEM)
VMEM = pl.BlockSpec(memory_space=pltpu.VMEM)


def add_group(lists_ref, which, at, size, psi, left, right, acc):
    tiles, width = acc.shape[1], acc.shape[-1]
    products = []
    for i in range(size):
        slot, source = lists_ref[which, 0, at + i], lists_ref[which, 1, at + i]
        block = psi[pl.ds(pl.multiple_of(source * width, width), width)]
        product = jnp.dot(left[slot], block, preferred_element_type=jnp.float32)
        products.append(product.astype(jnp.bfloat16))
    for i in range(size):
        slot, target = lists_ref[which, 0, at + i], lists_ref[which, 2, at + i]
        term = jnp.dot(products[i], right[slot], preferred_element_type=jnp.float32)
        term = term.reshape(tiles, 2, 8, width)
        for c in range(2):
            acc[c, :, target] += term[:, c]


def add_terms(which, lists_ref, counts_ref, psi, left, right, acc, ready=None):
    count = counts_ref[which]
    groups = (count + GROUP // 2 - 1) // GROUP

    def step(j, carry):
        if ready is not None:
            ready(j * GROUP, GROUP)
        add_group(lists_ref, which, j * GROUP, GROUP, psi, left, right, acc)
        return carry

    lax.fori_loop(0, groups, step, 0)

    @pl.when(count > groups * GROUP)
    def _():
        if ready is not None:
            ready(groups * GROUP, GROUP // 2)
        add_group(lists_ref, which, groups * GROUP, GROUP // 2, psi, left, right, acc)


def prepare_kernel(
    place_ref, live_ref, pairs_ref, own, left_ref, right_ref,
    lists_ref, counts_ref, left_here, right_here, acc, waited, left_sem, right_sem,
):
    part = left_ref.shape[0] // PARTS

    def loads(i):
        slots = pl.ds(i * part, part)
        return (
            pltpu.make_async_copy(left_ref.at[slots], left_here.at[slots], left_sem.at[i]),
            pltpu.make_async_copy(right_ref.at[slots], right_here.at[slots], right_sem.at[i]),
        )

    for i in range(PARTS):
        for load in loads(i):
            load.start()
    acc[...] = jnp.zeros_like(acc)
    core, layer = place_ref[0], place_ref[1]

    def clear(i, carry):
        for which in range(3):
            lists_ref[which, 0, i] = 0
            lists_ref[which, 1, i] = 0
            lists_ref[which, 2, i] = 8
        return carry

    lax.fori_loop(0, lists_ref.shape[2], clear, 0)
    for which in range(3):
        counts_ref[which] = 0

    def put(k, carry):
        ahead = (pairs_ref[0, k] - layer) & 7
        hops = jnp.minimum(ahead, 8 - ahead)
        theirs = 1 - ((ahead > 4).astype(jnp.int32) ^ core)
        which = jnp.where(hops == 0, 0, jnp.where(hops == 4, 2, 1 + theirs))
        source = jnp.where(hops == 0, 0, 4 - hops)
        at = counts_ref[which]
        lists_ref[which, 0, at] = k
        lists_ref[which, 1, at] = source
        lists_ref[which, 2, at] = pairs_ref[1, k]
        counts_ref[which] = at + 1
        return carry

    lax.fori_loop(0, live_ref[0], put, 0)
    waited[0] = 0

    def ready(at, size):
        last = lists_ref[0, 0, at]
        for i in range(1, size):
            last = jnp.maximum(last, lists_ref[0, 0, at + i])
        until = last // part + 1
        for i in range(PARTS):

            @pl.when((i >= waited[0]) & (i < until))
            def _():
                for load in loads(i):
                    load.wait()

        waited[0] = jnp.maximum(waited[0], until)

    add_terms(0, lists_ref, counts_ref, own, left_here, right_here, acc, ready)
    for i in range(PARTS):

        @pl.when(i >= waited[0])
        def _():
            for load in loads(i):
                load.wait()


def prepare(place, live, pairs, own, left, right):
    slots, rows, width = left.shape
    return pl.pallas_call(
        prepare_kernel,
        out_shape=(
            jax.ShapeDtypeStruct((3, 3, slots + GROUP), jnp.int32),
            jax.ShapeDtypeStruct((3,), jnp.int32),
            jax.ShapeDtypeStruct(left.shape, left.dtype),
            jax.ShapeDtypeStruct(right.shape, right.dtype),
            jax.ShapeDtypeStruct((2, rows // 16, 9, 8, width), jnp.float32),
        ),
        in_specs=[SMEM] * 3 + [VMEM] + [pl.BlockSpec(memory_space=pl.ANY)] * 2,
        out_specs=(SMEM, SMEM, VMEM, VMEM, VMEM),
        scratch_shapes=[
            pltpu.SMEM((1,), jnp.int32),
            pltpu.SemaphoreType.DMA((PARTS,)),
            pltpu.SemaphoreType.DMA((PARTS,)),
        ],
        compiler_params=pltpu.CompilerParams(vmem_limit_bytes=37 * 1024 * 1024),
        cost_estimate=pl.CostEstimate(
            flops=0, bytes_accessed=4 * (left.size + right.size), transcendentals=0
        ),
    )(place, live, pairs, own, left, right)


def middle_terms(which, lists, counts, blocks, left, right, before):
    def kernel(lists_ref, counts_ref, psi, left, right, before_ref, acc):
        add_terms(which, lists_ref, counts_ref, psi, left, right, acc)

    return pl.pallas_call(
        kernel,
        out_shape=jax.ShapeDtypeStruct(before.shape, before.dtype),
        in_specs=[SMEM] * 2 + [VMEM] * 4,
        out_specs=VMEM,
        input_output_aliases={5: 0},
        compiler_params=pltpu.CompilerParams(vmem_limit_bytes=16 * 1024 * 1024),
        cost_estimate=term_cost(left),
    )(lists, counts, blocks, left, right, before)


def last_kernel(
    place_ref, lists_ref, counts_ref, mine, other, left, right, before, keep_ref, send_ref, psi, acc
):
    core = place_ref[0]
    tiles, share, width = send_ref.shape
    half = width // 2
    own_rows = pl.ds(pl.multiple_of(core * half, half), half)
    their_rows = pl.ds(pl.multiple_of((1 - core) * half, half), half)
    psi[own_rows] = mine[:half]
    psi[their_rows] = other[:half]
    psi[width:] = other[width:]
    acc[...] = before[...]
    add_terms(2, lists_ref, counts_ref, psi, left, right, acc)
    for tile in range(tiles):
        keep_ref[tile] = acc[core, tile, :8].reshape(share, width)
        send_ref[tile] = acc[1 - core, tile, :8].reshape(share, width).astype(send_ref.dtype)


def term_cost(left):
    slots, rows, width = left.shape
    return pl.CostEstimate(
        flops=2 * rows * rows * width * slots,
        bytes_accessed=2 * rows * width * slots,
        transcendentals=0,
    )


def last_terms(place, lists, counts, mine, other, left, right, before):
    _, rows, width = left.shape
    tiles = rows // 16
    return pl.pallas_call(
        last_kernel,
        out_shape=(
            jax.ShapeDtypeStruct((tiles, 64, width), jnp.float32),
            jax.ShapeDtypeStruct((tiles, 64, width), jnp.bfloat16),
        ),
        in_specs=[SMEM] * 3 + [VMEM] * 5,
        out_specs=(VMEM, VMEM),
        scratch_shapes=[
            pltpu.VMEM((4 * rows, width), jnp.bfloat16),
            pltpu.VMEM((2, tiles, 9, 8, width), jnp.float32),
        ],
        compiler_params=pltpu.CompilerParams(vmem_limit_bytes=16 * 1024 * 1024),
        cost_estimate=term_cost(left),
    )(place, lists, counts, mine, other, left, right, before)


def fetch(value, shifts):
    moves = [
        (core * 8 + layer, core * 8 + (layer + shift) % 8)
        for core, shift in enumerate(shifts)
        for layer in range(8)
    ]
    return lax.ppermute(value, ("c", "z"), moves)


def body(wavefunction, block_rows, left_terms, right_terms, block_pairs, live_counts):
    _, rows, width = wavefunction.shape
    core = lax.axis_index("c").astype(jnp.int32)
    layer = lax.axis_index("z").astype(jnp.int32)
    place = jnp.stack([core, layer])
    half = rows // 2
    row_index = lax.broadcasted_iota(jnp.int32, (rows, 1), 0)
    own = jnp.where(row_index < block_rows[0], wavefunction[0], jnp.zeros_like(wavefunction[0]))
    own_half = jnp.where(core == 0, own[:half], own[half:])
    fetched = [fetch(own, (shift, -shift)) for shift in (3, 2, 1)]
    far = fetch(own_half, (4, 4))
    prepared = prepare(place, live_counts, block_pairs.T, own, left_terms, right_terms)
    fetched, far, prepared = lax.optimization_barrier((fetched, far, prepared))
    lists, counts, left, right, sums = prepared
    mine = jnp.concatenate([far, far, *fetched], 0)
    other = lax.ppermute(mine, "c", SWAP)
    sums = middle_terms(1, lists, counts, mine, left, right, sums)
    keep, send = last_terms(place, lists, counts, mine, other, left, right, sums)
    received = lax.ppermute(send, "c", SWAP)
    pair_sum = keep + received.astype(jnp.float32)
    pieces = lax.all_to_all(pair_sum.astype(jnp.bfloat16), LAYER, 0, 0)
    layer_sum = pieces.astype(jnp.float32).sum(0).reshape(8, 8, width)
    sigma = lax.all_to_all(layer_sum, "z", 0, 0).sum(0)
    own_tile = lax.axis_index(("y", "x", "c"))
    own_rows = own_tile * 8 + lax.broadcasted_iota(jnp.int32, (8, 1), 0)
    return jnp.where(own_rows < block_rows[0], sigma, jnp.zeros_like(sigma))[None]


def solution(mesh):
    devices = mesh.devices.reshape(4, 4, 2, mesh.shape["grp"])
    grid = Mesh(devices, ("y", "x", "c", "z"))
    everywhere = ("y", "x", "c", "z")
    placed = (
        P("z", None, None),
        P("z"),
        P(everywhere, None, None),
        P(everywhere, None, None),
        P(everywhere, None),
        P(everywhere),
    )
    return jax.shard_map(
        body, mesh=grid, in_specs=placed, out_specs=P("z", ("y", "x", "c"), None), check_vma=False
    )
```

```python
import jax
import jax.numpy as jnp
from jax import lax
from jax.experimental import pallas as pl
from jax.experimental.pallas import tpu as pltpu
from jax.sharding import Mesh, PartitionSpec as P

GROUP = 8
PARTS = 6
SWAP = [(0, 1), (1, 0)]
SMEM = pl.BlockSpec(memory_space=pltpu.SMEM)
VMEM = pl.BlockSpec(memory_space=pltpu.VMEM)


def add_group(lists_ref, which, at, size, psi, left, right, acc):
    tiles, width = acc.shape[1], acc.shape[-1]
    products = []
    for i in range(size):
        slot, source = lists_ref[which, 0, at + i], lists_ref[which, 1, at + i]
        block = psi[pl.ds(pl.multiple_of(source * width, width), width)]
        product = jnp.dot(left[slot], block, preferred_element_type=jnp.float32)
        products.append(product.astype(jnp.bfloat16))
    for i in range(size):
        slot, target = lists_ref[which, 0, at + i], lists_ref[which, 2, at + i]
        term = jnp.dot(products[i], right[slot], preferred_element_type=jnp.float32)
        term = term.reshape(tiles, 2, 8, width)
        for c in range(2):
            acc[c, :, target] += term[:, c]


def add_terms(which, lists_ref, counts_ref, psi, left, right, acc, ready=None):
    count = counts_ref[which]
    groups = (count + GROUP // 2 - 1) // GROUP

    def step(j, carry):
        if ready is not None:
            ready(j * GROUP, GROUP)
        add_group(lists_ref, which, j * GROUP, GROUP, psi, left, right, acc)
        return carry

    lax.fori_loop(0, groups, step, 0)

    @pl.when(count > groups * GROUP)
    def _():
        if ready is not None:
            ready(groups * GROUP, GROUP // 2)
        add_group(lists_ref, which, groups * GROUP, GROUP // 2, psi, left, right, acc)


def prepare_kernel(
    place_ref, live_ref, pairs_ref, own, left_ref, right_ref,
    lists_ref, counts_ref, left_here, right_here, acc, waited, left_sem, right_sem,
):
    part = left_ref.shape[0] // PARTS

    def loads(i):
        slots = pl.ds(i * part, part)
        return (
            pltpu.make_async_copy(left_ref.at[slots], left_here.at[slots], left_sem.at[i]),
            pltpu.make_async_copy(right_ref.at[slots], right_here.at[slots], right_sem.at[i]),
        )

    for i in range(PARTS):
        for load in loads(i):
            load.start()
    acc[...] = jnp.zeros_like(acc)
    core, layer = place_ref[0], place_ref[1]

    def clear(i, carry):
        for which in range(3):
            lists_ref[which, 0, i] = 0
            lists_ref[which, 1, i] = 0
            lists_ref[which, 2, i] = 8
        return carry

    lax.fori_loop(0, lists_ref.shape[2], clear, 0)
    for which in range(3):
        counts_ref[which] = 0

    def put(k, carry):
        ahead = (pairs_ref[0, k] - layer) & 7
        hops = jnp.minimum(ahead, 8 - ahead)
        theirs = 1 - ((ahead > 4).astype(jnp.int32) ^ core)
        which = jnp.where(hops == 0, 0, jnp.where(hops == 4, 2, 1 + theirs))
        source = jnp.where(hops == 0, 0, 4 - hops)
        at = counts_ref[which]
        lists_ref[which, 0, at] = k
        lists_ref[which, 1, at] = source
        lists_ref[which, 2, at] = pairs_ref[1, k]
        counts_ref[which] = at + 1
        return carry

    lax.fori_loop(0, live_ref[0], put, 0)
    waited[0] = 0

    def ready(at, size):
        last = lists_ref[0, 0, at]
        for i in range(1, size):
            last = jnp.maximum(last, lists_ref[0, 0, at + i])
        until = last // part + 1
        for i in range(PARTS):

            @pl.when((i >= waited[0]) & (i < until))
            def _():
                for load in loads(i):
                    load.wait()

        waited[0] = jnp.maximum(waited[0], until)

    add_terms(0, lists_ref, counts_ref, own, left_here, right_here, acc, ready)
    for i in range(PARTS):

        @pl.when(i >= waited[0])
        def _():
            for load in loads(i):
                load.wait()


def prepare(place, live, pairs, own, left, right):
    slots, rows, width = left.shape
    return pl.pallas_call(
        prepare_kernel,
        out_shape=(
            jax.ShapeDtypeStruct((3, 3, slots + GROUP), jnp.int32),
            jax.ShapeDtypeStruct((3,), jnp.int32),
            jax.ShapeDtypeStruct(left.shape, left.dtype),
            jax.ShapeDtypeStruct(right.shape, right.dtype),
            jax.ShapeDtypeStruct((2, rows // 16, 9, 8, width), jnp.float32),
        ),
        in_specs=[SMEM] * 3 + [VMEM] + [pl.BlockSpec(memory_space=pl.ANY)] * 2,
        out_specs=(SMEM, SMEM, VMEM, VMEM, VMEM),
        scratch_shapes=[
            pltpu.SMEM((1,), jnp.int32),
            pltpu.SemaphoreType.DMA((PARTS,)),
            pltpu.SemaphoreType.DMA((PARTS,)),
        ],
        compiler_params=pltpu.CompilerParams(vmem_limit_bytes=37 * 1024 * 1024),
        cost_estimate=pl.CostEstimate(
            flops=0, bytes_accessed=4 * (left.size + right.size), transcendentals=0
        ),
    )(place, live, pairs, own, left, right)


def middle_terms(which, lists, counts, blocks, left, right, before):
    def kernel(lists_ref, counts_ref, psi, left, right, before_ref, acc):
        add_terms(which, lists_ref, counts_ref, psi, left, right, acc)

    return pl.pallas_call(
        kernel,
        out_shape=jax.ShapeDtypeStruct(before.shape, before.dtype),
        in_specs=[SMEM] * 2 + [VMEM] * 4,
        out_specs=VMEM,
        input_output_aliases={5: 0},
        compiler_params=pltpu.CompilerParams(vmem_limit_bytes=16 * 1024 * 1024),
        cost_estimate=term_cost(left),
    )(lists, counts, blocks, left, right, before)


def last_kernel(
    place_ref, lists_ref, counts_ref, mine, other, left, right, before, keep_ref, send_ref, psi, acc
):
    core = place_ref[0]
    tiles, share, width = send_ref.shape
    half = width // 2
    own_rows = pl.ds(pl.multiple_of(core * half, half), half)
    their_rows = pl.ds(pl.multiple_of((1 - core) * half, half), half)
    psi[own_rows] = mine[:half]
    psi[their_rows] = other[:half]
    psi[width:] = other[width:]
    acc[...] = before[...]
    add_terms(2, lists_ref, counts_ref, psi, left, right, acc)
    for tile in range(tiles):
        keep_ref[tile] = acc[core, tile, :8].reshape(share, width)
        send_ref[tile] = acc[1 - core, tile, :8].reshape(share, width).astype(send_ref.dtype)


def term_cost(left):
    slots, rows, width = left.shape
    return pl.CostEstimate(
        flops=2 * rows * rows * width * slots,
        bytes_accessed=2 * rows * width * slots,
        transcendentals=0,
    )


def last_terms(place, lists, counts, mine, other, left, right, before):
    _, rows, width = left.shape
    tiles = rows // 16
    return pl.pallas_call(
        last_kernel,
        out_shape=(
            jax.ShapeDtypeStruct((tiles, 64, width), jnp.float32),
            jax.ShapeDtypeStruct((tiles, 64, width), jnp.bfloat16),
        ),
        in_specs=[SMEM] * 3 + [VMEM] * 5,
        out_specs=(VMEM, VMEM),
        scratch_shapes=[
            pltpu.VMEM((4 * rows, width), jnp.bfloat16),
            pltpu.VMEM((2, tiles, 9, 8, width), jnp.float32),
        ],
        compiler_params=pltpu.CompilerParams(vmem_limit_bytes=16 * 1024 * 1024),
        cost_estimate=term_cost(left),
    )(place, lists, counts, mine, other, left, right, before)


def fetch(value, shifts):
    moves = [
        (core * 8 + layer, core * 8 + (layer + shift) % 8)
        for core, shift in enumerate(shifts)
        for layer in range(8)
    ]
    return lax.ppermute(value, ("c", "z"), moves)


def body(wavefunction, block_rows, left_terms, right_terms, block_pairs, live_counts):
    _, rows, width = wavefunction.shape
    core = lax.axis_index("c").astype(jnp.int32)
    layer = lax.axis_index("z").astype(jnp.int32)
    place = jnp.stack([core, layer])
    half = rows // 2
    row_index = lax.broadcasted_iota(jnp.int32, (rows, 1), 0)
    own = jnp.where(row_index < block_rows[0], wavefunction[0], jnp.zeros_like(wavefunction[0]))
    own_half = jnp.where(core == 0, own[:half], own[half:])
    fetched = [fetch(own, (shift, -shift)) for shift in (3, 2, 1)]
    far = fetch(own_half, (4, 4))
    prepared = prepare(place, live_counts, block_pairs.T, own, left_terms, right_terms)
    fetched, far, prepared = lax.optimization_barrier((fetched, far, prepared))
    lists, counts, left, right, sums = prepared
    mine = jnp.concatenate([far, far, *fetched], 0)
    other = lax.ppermute(mine, "c", SWAP)
    sums = middle_terms(1, lists, counts, mine, left, right, sums)
    keep, send = last_terms(place, lists, counts, mine, other, left, right, sums)
    received = lax.ppermute(send, "c", SWAP)
    pair_sum = (keep + received.astype(jnp.float32)).reshape(4, 256, width)
    line = lax.axis_index("y")

    def piece(shift):
        return lax.dynamic_index_in_dim(pair_sum, (line + shift) % 4, 0, False)

    line_sum = piece(0)
    for shift in (2, 1, 3):
        moves = [(i, (i + shift) % 4) for i in range(4)]
        arrived = lax.ppermute(piece(shift).astype(jnp.bfloat16), "y", moves)
        line_sum += arrived.astype(jnp.float32)
    line_sum = line_sum.reshape(32, 8, width)
    pieces = lax.all_to_all(line_sum.astype(jnp.bfloat16), ("x", "z"), 0, 0)
    sigma = pieces.astype(jnp.float32).sum(0)
    own_tile = lax.axis_index(("y", "x", "c"))
    own_rows = own_tile * 8 + lax.broadcasted_iota(jnp.int32, (8, 1), 0)
    return jnp.where(own_rows < block_rows[0], sigma, jnp.zeros_like(sigma))[None]


def solution(mesh):
    devices = mesh.devices.reshape(4, 4, 2, mesh.shape["grp"])
    grid = Mesh(devices, ("y", "x", "c", "z"))
    everywhere = ("y", "x", "c", "z")
    placed = (
        P("z", None, None),
        P("z"),
        P(everywhere, None, None),
        P(everywhere, None, None),
        P(everywhere, None),
        P(everywhere),
    )
    return jax.shard_map(
        body, mesh=grid, in_specs=placed, out_specs=P("z", ("y", "x", "c"), None), check_vma=False
    )
```
